256 devices in a mesh: span: 16 (over y, z_lo), seq: 16 (over z_hi, x, core).
Axes of the slice: x: 4, y: 4, z: 8 (z_hi: 2, z_lo: 4; z = z_hi * 4 + z_lo), core: 2. Of those that a mesh axis runs over, the one named last changes fastest.
Arguments:
- qkv: bfloat16 [16, 2048, 3, 4096], P('span', 'seq'), may hold values from -10 to 10
- timestep: int32 [16], P('span'), may hold values from 0 to 49
- offsets: int32 [16], P('span'), may hold values from 0 to 13, as said below
- gate_table: float32 [50, 4096], replicated, may hold values from 0.5 to 4
Outputs:
- attended: bfloat16 [16, 2048, 4096], P('span', 'seq')
The draws below stay inside these ranges and needn't reach their ends.
Inputs may be any that keep to these rules, and one draw needn't show every extreme that they name: max(0, c - 2) <= offsets[c] <= min(c, 13); the last span has offsets equal to 13.
All inputs are finite; a program needn't handle non-finite values.
Results may differ from the reference program's by a relative error of at most 0.0031.
Values may be sent and summed in bfloat16 or wider, within the bound.
A program may use at most 128 MiB of HBM per device.

```python
import math
import jax
import jax.numpy as jnp
from jax import lax

HD = 128
WIN = 2
STEPS = 50
HEADS = 32
SPANS = 16
CTOK = 2048


def draw_qkv(key, part):
    key = jax.random.fold_in(key, 11)
    key_base = jax.random.fold_in(key, 0)
    full_shape = (SPANS, CTOK, 3, HEADS * HD)
    spread = jnp.array([1.6, 1.6, 1.0], jnp.float32).reshape(1, 1, 3, 1)
    base_draw = jax.random.normal(key_base, full_shape, jnp.float32) * spread
    return jnp.clip(base_draw, -6.0, 6.0).astype(jnp.bfloat16)


def draw_offsets(key, part):
    key = jax.random.fold_in(key, 23)
    going_back = jax.random.randint(key, (SPANS,), 0, WIN + 1)
    span_ids = jnp.arange(SPANS, dtype=jnp.int32)
    going_back = jnp.where(span_ids == SPANS - 1, WIN, going_back)
    first_allowed = jnp.minimum(span_ids - going_back, SPANS - 1 - WIN)
    return jnp.maximum(first_allowed, 0).astype(jnp.int32)


def plant(values, rng, least, largest):
    index_at = [jax.random.randint(jax.random.fold_in(rng, axis), (), 0, length) for axis, length in enumerate(values.shape)]
    main_axis = values.shape.index(max(values.shape))
    next_to = index_at[:main_axis] + [(index_at[main_axis] + 1) % values.shape[main_axis]] + index_at[main_axis + 1:]
    return values.at[tuple(index_at)].set(least).at[tuple(next_to)].set(largest)


def setup_inputs(seed: int = 0) -> dict:
    splits = jax.random.split(jax.random.key(seed), 5)
    return {
        "qkv": draw_qkv(jax.random.fold_in(splits[4], 71), 0),
        "timestep": plant(jax.random.randint(splits[1], (SPANS,), 0, STEPS), jax.random.fold_in(splits[1], 1), 0, STEPS - 1).astype(jnp.int32),
        "offsets": draw_offsets(jax.random.fold_in(splits[4], 71), 0),
        "gate_table": jnp.clip(jnp.exp(jax.random.uniform(splits[3], (STEPS, HEADS * HD), jnp.float32, math.log(0.5), math.log(4.0))), 0.5, 4.0),
    }


def span_output(span_index, qkv, offsets, timestep, gate_table):
    scale_factor = 1.0 / math.sqrt(HD)
    queries = qkv[span_index, :, 0, :].reshape(CTOK, HEADS, HD).astype(jnp.float32)

    def block_scores(source):
        key_rows = qkv[source, :, 1, :].reshape(CTOK, HEADS, HD).astype(jnp.float32)
        value_rows = qkv[source, :, 2, :].reshape(CTOK, HEADS, HD).astype(jnp.float32)
        scores = jnp.einsum('qhd,khd->hqk', queries, key_rows) * scale_factor
        return (scores, value_rows)

    def weighted(probabilities, value_rows):
        rounded = lax.optimization_barrier(probabilities.astype(jnp.bfloat16))
        return jnp.einsum('hqk,khd->hqd', rounded.astype(jnp.float32), value_rows)
    scores, value_rows = block_scores(span_index)
    running = lax.optimization_barrier(jnp.max(scores, axis=2, keepdims=True))
    probabilities = jnp.exp(scores - running)
    denominator = lax.optimization_barrier(jnp.sum(probabilities, axis=2, keepdims=True))
    numerator = weighted(probabilities, value_rows)
    for distance in range(1, WIN + 1):
        source = span_index - distance
        allowed = (source >= offsets[span_index]) & (source >= 0)
        scores, value_rows = block_scores(jnp.maximum(source, 0))
        newmax = jnp.maximum(running, lax.optimization_barrier(jnp.max(scores, axis=2, keepdims=True)))
        factor = jnp.exp(running - newmax)
        probabilities = jnp.exp(scores - newmax)
        new_denominator = denominator * factor + lax.optimization_barrier(jnp.sum(probabilities, axis=2, keepdims=True))
        new_numerator = numerator * factor + weighted(probabilities, value_rows)
        running = jnp.where(allowed, newmax, running)
        denominator = jnp.where(allowed, new_denominator, denominator)
        numerator = jnp.where(allowed, new_numerator, numerator)
    gate_row = gate_table[timestep[span_index]].reshape(HEADS, 1, HD)
    result = numerator / denominator * gate_row
    return jnp.transpose(result, (1, 0, 2)).reshape(CTOK, HEADS * HD).astype(jnp.bfloat16)

def reference(qkv, timestep, offsets, gate_table):
    return lax.map(lambda span_index: span_output(span_index, qkv, offsets, timestep, gate_table), jnp.arange(SPANS, dtype=jnp.int32))
```

```python
import functools
import math

import jax
import jax.numpy as jnp
from jax import lax
from jax.experimental import pallas as pl
from jax.experimental.pallas import tpu as pltpu
from jax.sharding import PartitionSpec as P

HD = 128
WIN = 2
SLOTS = WIN + 1
PAIR = 2
TOK = 128
LANES = 8
HALF = LANES * TOK
ROWS = 2 * HALF
SCALE = math.log2(math.e) / math.sqrt(HD)
MESH = pl.DeviceIdType.MESH


def device(y, z, xc):
    return (y * 4 + z % 4, (z // 4) * 8 + xc)


def kernel(
    qkv, timestep, offsets, gate_table, out,
    queries, pairs, results, gates, row_max, row_sum, total,
    pair_recv, query_recv, out_recv, gate_sem,
    near_send, far_send, query_near_send, query_far_send, chain_send, out_near_send, out_far_send,
):
    span = lax.axis_index("span")
    seq = lax.axis_index("seq")
    y, z_lo = span // 4, span % 4
    z_hi, xc = seq // 8, seq % 8
    z = z_hi * 4 + z_lo
    group = (z_hi + y) % 2

    across = (z + 4) % 8
    drop_y, drop_z = (y + z_lo // 2) % 4, (z + 6) % 8
    source_y, source_z = (y + 3 + z_lo // 2) % 4, (z + 2) % 8
    following = device((y + (z_lo + 1) // 4) % 4, (z + 1) % 8, xc)
    previous = device((y + 3 + (z_lo + 3) // 4) % 4, (z + 7) % 8, xc)

    barrier = pltpu.get_barrier_semaphore()
    greeted = [following, previous]
    for turn in range(LANES):
        lane = (xc + turn) % LANES
        if turn:
            greeted.append(device(y, z, lane))
        greeted.append(device(y, across, lane))
        greeted.append(device(drop_y, drop_z, lane))
        greeted.append(device(source_y, source_z, lane))
    for other in greeted:
        pl.semaphore_signal(barrier, inc=1, device_id=other, device_id_type=MESH)
    pl.semaphore_wait(barrier, len(greeted))

    own_rows = pl.ds(pl.multiple_of(xc * TOK, TOK), TOK)
    far_rows = pl.ds(pl.multiple_of(HALF + xc * TOK, TOK), TOK)

    def columns(lane, which, head):
        return pl.ds(pl.multiple_of((lane * 2 + which) * (PAIR * HD) + head * HD, HD), HD)

    def send(src, dst, send_sem, recv_sem, target):
        pltpu.make_async_remote_copy(
            src_ref=src, dst_ref=dst, send_sem=send_sem, recv_sem=recv_sem,
            device_id=target, device_id_type=MESH,
        ).start()

    def wait_bytes(ref, sem):
        pltpu.make_async_copy(ref, ref, sem).wait()

    def scatter(head):
        for turn in range(LANES):
            lane = (xc + turn) % LANES
            send(
                qkv.at[1:3, :, columns(lane, 1 - group, head)],
                pairs.at[head, 2, 1, :, own_rows, :],
                far_send.at[head], pair_recv.at[head, 2, 1], device(drop_y, drop_z, lane),
            )
        for turn in range(LANES):
            lane = (xc + turn) % LANES
            src = qkv.at[1:3, :, columns(lane, group, head)]
            dst = pairs.at[head, 0, 0, :, own_rows, :]
            if turn:
                send(src, dst, near_send.at[head], pair_recv.at[head, 0, 0], device(y, z, lane))
            else:
                pltpu.make_async_copy(src, dst, pair_recv.at[head, 0, 0]).start()
        for turn in range(LANES):
            lane = (xc + turn) % LANES
            send(
                qkv.at[0, :, columns(lane, 1 - group, head)],
                queries.at[head, far_rows, :],
                query_far_send.at[head], query_recv.at[head], device(y, across, lane),
            )
        for turn in range(LANES):
            lane = (xc + turn) % LANES
            src = qkv.at[0, :, columns(lane, group, head)]
            dst = queries.at[head, own_rows, :]
            if turn:
                send(src, dst, query_near_send.at[head], query_recv.at[head], device(y, z, lane))
            else:
                pltpu.make_async_copy(src, dst, query_recv.at[head]).start()

    def arrived(head, slot, half):
        wait_bytes(pairs.at[head, slot, half], pair_recv.at[head, slot, half])

    def pass_on(head, slot, half):
        arrived(head, slot, half)
        to = slot + 1 if half == 0 else slot - 1
        send(
            pairs.at[head, slot, half], pairs.at[head, to, half],
            chain_send.at[head, slot, half], pair_recv.at[head, to, half],
            following if half == 0 else previous,
        )

    def attend(head, slot, half, part):
        rows = pl.ds(part * HALF, HALF)
        scores = lax.dot_general(
            queries[head, rows, :], pairs[head, slot, half, 0],
            (((1,), (1,)), ((), ())), preferred_element_type=jnp.float32,
        )
        old = row_max[head, rows, :]
        new = jnp.maximum(old, jnp.broadcast_to(jnp.max(scores, axis=1, keepdims=True), old.shape))
        scale, shift = jnp.float32(SCALE), new * SCALE
        if slot:
            allowed = span - slot >= offsets[0]
            new = jnp.where(allowed, new, old)
            scale = jnp.where(allowed, scale, 0.0)
            shift = jnp.where(allowed, shift, 1e30)
        factor = jnp.exp2((old - new) * SCALE)
        weights = jnp.exp2(scores * scale - shift[:, :1])
        partial = weights[:, :HD]
        for block in range(1, HALF // HD):
            partial = partial + weights[:, block * HD : (block + 1) * HD]
        row_sum[head, rows, :] = row_sum[head, rows, :] * factor + partial
        total[head, rows, :] = total[head, rows, :] * factor + jnp.dot(
            weights.astype(jnp.bfloat16), pairs[head, slot, half, 1], preferred_element_type=jnp.float32
        )
        row_max[head, rows, :] = new

    def attend_all(head, slot, half):
        def step(part, carry):
            attend(head, slot, half, part)
            return carry

        lax.fori_loop(0, 2, step, 0)

    def finish(head, part):
        rows = pl.ds(part * HALF, HALF)
        row = lax.broadcasted_iota(jnp.int32, gates.shape, 0) == timestep[0]
        gate = jnp.sum(jnp.where(row, gates[...], 0.0), axis=0, keepdims=True)[:, head * HD : (head + 1) * HD]
        denominator = jnp.sum(row_sum[head, rows, :], axis=1, keepdims=True)
        results[head, rows, :] = (total[head, rows, :] / denominator * gate).astype(jnp.bfloat16)
        for turn in range(LANES):
            lane = (xc + turn) % LANES
            src = results.at[head, pl.ds(pl.multiple_of(part * HALF + lane * TOK, TOK), TOK), :]
            dst = out.at[:, columns(xc, group, head)]
            if part:
                send(src, dst, out_far_send.at[head], out_recv, device(y, across, lane))
            elif turn:
                send(src, dst, out_near_send.at[head], out_recv, device(y, z, lane))
            else:
                pltpu.make_async_copy(src, dst, out_recv).start()

    def finish_with(head, slot, half):
        for part in (1, 0):
            attend(head, slot, half, part)
            finish(head, part)

    gate_copy = pltpu.make_async_copy(
        gate_table.at[:, pl.ds(pl.multiple_of((xc * 2 + group) * (PAIR * HD), PAIR * HD), PAIR * HD)], gates, gate_sem
    )
    scatter(0)
    scatter(1)
    gate_copy.start()
    row_max[...] = jnp.full_like(row_max, -1e30)
    row_sum[...] = jnp.zeros_like(row_sum)
    total[...] = jnp.zeros_like(total)
    gate_copy.wait()

    pass_on(0, 0, 0)
    pass_on(0, 2, 1)
    pass_on(1, 0, 0)
    wait_bytes(queries.at[0], query_recv.at[0])
    attend_all(0, 0, 0)
    pass_on(0, 1, 0)
    pass_on(0, 1, 1)
    attend_all(0, 2, 1)
    pass_on(1, 2, 1)
    attend_all(0, 1, 0)
    pass_on(1, 1, 0)
    attend_all(0, 1, 1)
    pass_on(1, 1, 1)
    arrived(0, 2, 0)
    attend_all(0, 2, 0)
    wait_bytes(queries.at[1], query_recv.at[1])
    attend_all(1, 0, 0)
    arrived(0, 0, 1)
    finish_with(0, 0, 1)
    attend_all(1, 2, 1)
    attend_all(1, 1, 0)
    attend_all(1, 1, 1)
    arrived(1, 2, 0)
    attend_all(1, 2, 0)
    arrived(1, 0, 1)
    finish_with(1, 0, 1)

    for head in range(PAIR):
        wait_bytes(pairs.at[head, 0, 0], far_send.at[head])
        wait_bytes(pairs.at[head, 0, 0, :, : HALF - TOK, :], near_send.at[head])
        wait_bytes(queries.at[head, :HALF, :], query_far_send.at[head])
        wait_bytes(queries.at[head, : HALF - TOK, :], query_near_send.at[head])
        for slot, half in ((0, 0), (1, 0), (1, 1), (2, 1)):
            wait_bytes(pairs.at[head, slot, half], chain_send.at[head, slot, half])
        wait_bytes(results.at[head, :HALF, :], out_far_send.at[head])
        wait_bytes(results.at[head, : HALF - TOK, :], out_near_send.at[head])
    wait_bytes(out, out_recv)


def body(qkv, timestep, offsets, gate_table):
    stacked = jnp.transpose(qkv[0], (1, 0, 2))
    anywhere = pl.BlockSpec(memory_space=pl.ANY)
    scalar = pl.BlockSpec(memory_space=pltpu.SMEM)
    dma = pltpu.SemaphoreType.DMA
    out = pl.pallas_call(
        kernel,
        out_shape=jax.ShapeDtypeStruct((TOK, qkv.shape[3]), jnp.bfloat16),
        in_specs=[anywhere, scalar, scalar, anywhere],
        out_specs=anywhere,
        scratch_shapes=[
            pltpu.VMEM((PAIR, ROWS, HD), jnp.bfloat16),
            pltpu.VMEM((PAIR, SLOTS, 2, 2, HALF, HD), jnp.bfloat16),
            pltpu.VMEM((PAIR, ROWS, HD), jnp.bfloat16),
            pltpu.VMEM((gate_table.shape[0], PAIR * HD), jnp.float32),
            pltpu.VMEM((PAIR, ROWS, HD), jnp.float32),
            pltpu.VMEM((PAIR, ROWS, HD), jnp.float32),
            pltpu.VMEM((PAIR, ROWS, HD), jnp.float32),
            dma((PAIR, SLOTS, 2)),
            dma((PAIR,)),
            dma,
            dma,
            dma((PAIR,)),
            dma((PAIR,)),
            dma((PAIR,)),
            dma((PAIR,)),
            dma((PAIR, SLOTS, 2)),
            dma((PAIR,)),
            dma((PAIR,)),
        ],
        compiler_params=pltpu.CompilerParams(
            collective_id=0, has_side_effects=True, vmem_limit_bytes=56 * 1024 * 1024
        ),
        cost_estimate=pl.CostEstimate(
            flops=4 * PAIR * ROWS * SLOTS * ROWS * HD,
            bytes_accessed=4 * 1024 * 1024,
            transcendentals=PAIR * ROWS * SLOTS * ROWS,
        ),
        name="span_attention",
    )(stacked, timestep, offsets, gate_table)
    return out[None]


def solution(mesh):
    return jax.shard_map(
        body,
        mesh=mesh,
        in_specs=(P("span", "seq", None, None), P("span"), P("span"), P()),
        out_specs=P("span", "seq", None),
        check_vma=False,
    )
```

```python
import math

import jax
import jax.numpy as jnp
from jax import lax
from jax.experimental import pallas as pl
from jax.experimental.pallas import tpu as pltpu
from jax.sharding import PartitionSpec as P

HD = 128
WIN = 2
OWN = 2
SLOTS = OWN + WIN
SOURCES = 16
TOK = 128
ROWS = SOURCES * TOK
CHIPS = 32
PARTS = 2
PART = TOK // PARTS
KEYS = SOURCES * PART
TILE = 256
SCALE = math.log2(math.e) / math.sqrt(HD)
MESH = pl.DeviceIdType.MESH


def device(y, z, x, core):
    return (y * 4 + z % 4, (z // 4) * 8 + x * 2 + core)


def kernel(
    qkv, timestep, offsets, gate_table, out,
    queries, pairs, results, gates, note, notes, row_max, total,
    query_recv, pair_recv, out_recv, note_recv, gate_sem,
    query_send, pair_send, out_send, note_send, chain_send,
    query_near_send, pair_near_send, out_near_send,
):
    span = lax.axis_index("span")
    seq = lax.axis_index("seq")
    y, z_lo = span // 4, span % 4
    z_hi, x, core = seq // 8, seq // 2 % 4, seq % 2
    z = z_hi * 4 + z_lo
    head = x * 8 + z
    home = z_lo // 2
    first_span = y * 4 + core * OWN
    at_home = core == home
    following = device((y + core) % 4, z, x, 1 - core)
    beyond = device((y + 3 + 2 * core) % 4, z, x, 1 - core)

    barrier = pltpu.get_barrier_semaphore()
    greeted = [beyond]
    for turn in range(CHIPS):
        for other in range(2):
            if turn or other:
                greeted.append(device(y, (z + turn) % 8, (x + turn // 8) % 4, (core + other) % 2))
    for other in greeted:
        pl.semaphore_signal(barrier, inc=1, device_id=other, device_id_type=MESH)
    pl.semaphore_wait(barrier, len(greeted))

    def columns(which):
        return pl.ds(pl.multiple_of(which * HD, HD), HD)

    def remote(src, dst, send_sem, recv_sem, target):
        return pltpu.make_async_remote_copy(
            src_ref=src, dst_ref=dst, send_sem=send_sem, recv_sem=recv_sem,
            device_id=target, device_id_type=MESH,
        )

    def here_or_there(stays, src, dst, send_sem, recv_sem, target):
        @pl.when(stays)
        def _():
            pltpu.make_async_copy(src, dst, recv_sem).start()

        @pl.when(jnp.logical_not(stays))
        def _():
            remote(src, dst, send_sem, recv_sem, target).start()

    def wait_bytes(ref, sem):
        pltpu.make_async_copy(ref, ref, sem).wait()

    def scatter(source, dst, send_sem, near_sem, recv_sem):
        here_or_there(at_home, source(head), dst, near_sem, recv_sem, device(y, z, x, home))

        def step(turn, carry):
            to_z, to_x = (z + turn) % 8, (x + turn // 8) % 4
            remote(source(to_x * 8 + to_z), dst, send_sem, recv_sem, device(y, to_z, to_x, home)).start()
            return carry

        lax.fori_loop(1, CHIPS, step, 0)

    mine = z_lo % 2
    def scatter_queries():
        scatter(
            lambda which: qkv.at[0, :, columns(which)],
            queries.at[mine, pl.ds(pl.multiple_of(seq * TOK, TOK), TOK), :],
            query_send, query_near_send, query_recv.at[mine],
        )

    def scatter_pairs(part):
        scatter(
            lambda which: qkv.at[1:3, pl.ds(part * PART, PART), columns(which)],
            pairs.at[WIN + mine, part, :, pl.ds(pl.multiple_of(seq * PART, PART), PART), :],
            pair_send.at[part], pair_near_send.at[part], pair_recv.at[WIN + mine, part],
        )

    def pass_on(own, part):
        wait_bytes(pairs.at[WIN + own, part], pair_recv.at[WIN + own, part])
        remote(
            pairs.at[WIN + own, part], pairs.at[own, part],
            chain_send.at[own, part], pair_recv.at[own, part], following,
        ).start()

    def attend(own, slot, part):
        allowed = first_span + slot - WIN >= notes[own, 1, 0:1, 0:1]
        scale = jnp.where(allowed, jnp.float32(SCALE), 0.0)
        keys = pairs[slot, part, 0]
        values = jnp.concatenate([pairs[slot, part, 1], jnp.ones((KEYS, HD), jnp.bfloat16)], axis=1)

        def rows(tile):
            return pl.ds(tile * TILE, TILE)

        def scores_of(tile):
            return lax.dot_general(
                queries[own, rows(tile), :], keys, (((1,), (1,)), ((), ())), preferred_element_type=jnp.float32
            )

        def update(tile, scores):
            old = row_max[own, rows(tile), :]
            new = jnp.maximum(old, jnp.broadcast_to(jnp.max(scores, axis=1, keepdims=True), old.shape))
            new = jnp.where(allowed, new, old)
            factor = jnp.exp2((old - new) * SCALE)
            shift = jnp.where(allowed, new * SCALE, 1e30)
            weights = jnp.exp2(scores * scale - shift[:, :1]).astype(jnp.bfloat16)
            total[own, rows(tile), :] = total[own, rows(tile), :] * jnp.concatenate([factor, factor], axis=1) + jnp.dot(
                weights, values, preferred_element_type=jnp.float32
            )
            row_max[own, rows(tile), :] = new

        scores = scores_of(0)
        for tile in range(ROWS // TILE):
            later = scores_of(tile + 1) if tile + 1 < ROWS // TILE else None
            update(tile, scores)
            scores = later

    def finish(own):
        row = lax.broadcasted_iota(jnp.int32, gates.shape, 0) == notes[own, 0, 0:1, 0:1]
        gate = jnp.sum(jnp.where(row, gates[...], 0.0), axis=0, keepdims=True)
        results[own] = (total[own, :, :HD] / total[own, :, HD:] * gate).astype(jnp.bfloat16)
        to_z_lo = core * OWN + own

        def block(which):
            return results.at[own, pl.ds(pl.multiple_of(which * TOK, TOK), TOK), :]

        dst = out.at[:, columns(head)]
        here_or_there(
            z_lo == to_z_lo, block(seq), dst, out_near_send.at[own], out_recv, device(y, z_hi * 4 + to_z_lo, x, core)
        )

        def step(turn, carry):
            which = (seq + turn) % SOURCES
            target = device(y, which // 8 * 4 + to_z_lo, which // 2 % 4, which % 2)
            remote(block(which), dst, out_send.at[own], out_recv, target).start()
            return carry

        lax.fori_loop(1, SOURCES, step, 0)

    note[0] = jnp.full(note.shape[1:], timestep[0], jnp.int32)
    note[1] = jnp.full(note.shape[1:], offsets[0], jnp.int32)
    gate_copy = pltpu.make_async_copy(gate_table.at[:, columns(head)], gates, gate_sem)
    for other in range(2):
        to_z = z_hi * 4 + core * 2 + other
        here_or_there(
            jnp.logical_and(at_home, to_z == z), note, notes.at[mine],
            note_send.at[other], note_recv.at[mine], device(y, to_z, x, home),
        )
    scatter_queries()
    for part in range(PARTS):
        scatter_pairs(part)
    gate_copy.start()
    row_max[...] = jnp.full_like(row_max, -1e30)
    total[...] = jnp.zeros_like(total)
    gate_copy.wait()
    for own in range(OWN):
        wait_bytes(notes.at[own], note_recv.at[own])
        wait_bytes(queries.at[own], query_recv.at[own])

    def stage(index, carry):
        part, block = index // 6, index % 6
        own = 1 - block // 3
        slot = own + WIN - block % 3

        @pl.when(block == 0)
        def _():
            pass_on(1, part)
            pass_on(0, part)

        @pl.when(block == 2)
        def _():
            wait_bytes(pairs.at[1, part], pair_recv.at[1, part])

        @pl.when(block == 4)
        def _():
            wait_bytes(pairs.at[0, part], pair_recv.at[0, part])

        attend(own, slot, part)

        @pl.when(jnp.logical_and(part == PARTS - 1, block % 3 == 2))
        def _():
            finish(own)

        return carry

    lax.fori_loop(0, PARTS * 6, stage, 0)

    wait_bytes(queries.at[:, : ROWS - TOK // 2, :], query_send)
    for part in range(PARTS):
        wait_bytes(pairs.at[:2, part, :, : KEYS - PART // 2, :], pair_send.at[part])
        for own in range(OWN):
            wait_bytes(pairs.at[own, part], chain_send.at[own, part])
    for own in range(OWN):
        wait_bytes(results.at[own, : ROWS - TOK, :], out_send.at[own])

        @pl.when(z_lo != core * OWN + own)
        def _():
            wait_bytes(results.at[own, :TOK, :], out_near_send.at[own])

    for other in range(2):
        @pl.when(jnp.logical_not(jnp.logical_and(at_home, z_hi * 4 + core * 2 + other == z)))
        def _():
            wait_bytes(note, note_send.at[other])

    @pl.when(jnp.logical_not(at_home))
    def _():
        wait_bytes(queries.at[0, :TOK, :], query_near_send)
        for part in range(PARTS):
            wait_bytes(pairs.at[0, part, :, :PART, :], pair_near_send.at[part])

    wait_bytes(out, out_recv)


def body(qkv, timestep, offsets, gate_table):
    stacked = jnp.transpose(qkv[0], (1, 0, 2))
    anywhere = pl.BlockSpec(memory_space=pl.ANY)
    scalar = pl.BlockSpec(memory_space=pltpu.SMEM)
    dma = pltpu.SemaphoreType.DMA
    out = pl.pallas_call(
        kernel,
        out_shape=jax.ShapeDtypeStruct((TOK, qkv.shape[3]), jnp.bfloat16),
        in_specs=[anywhere, scalar, scalar, anywhere],
        out_specs=anywhere,
        scratch_shapes=[
            pltpu.VMEM((OWN, ROWS, HD), jnp.bfloat16),
            pltpu.VMEM((SLOTS, PARTS, 2, KEYS, HD), jnp.bfloat16),
            pltpu.VMEM((OWN, ROWS, HD), jnp.bfloat16),
            pltpu.VMEM((gate_table.shape[0], HD), jnp.float32),
            pltpu.VMEM((2, 8, HD), jnp.int32),
            pltpu.VMEM((OWN, 2, 8, HD), jnp.int32),
            pltpu.VMEM((OWN, ROWS, HD), jnp.float32),
            pltpu.VMEM((OWN, ROWS, 2 * HD), jnp.float32),
            dma((OWN,)),
            dma((SLOTS, PARTS)),
            dma,
            dma((OWN,)),
            dma,
            dma,
            dma((PARTS,)),
            dma((OWN,)),
            dma((2,)),
            dma((OWN, PARTS)),
            dma,
            dma((PARTS,)),
            dma((OWN,)),
        ],
        compiler_params=pltpu.CompilerParams(
            collective_id=0, has_side_effects=True, vmem_limit_bytes=56 * 1024 * 1024
        ),
        cost_estimate=pl.CostEstimate(
            flops=4 * OWN * ROWS * (WIN + 1) * ROWS * HD,
            bytes_accessed=4 * 1024 * 1024,
            transcendentals=OWN * ROWS * (WIN + 1) * ROWS,
        ),
        name="span_attention",
    )(stacked, timestep, offsets, gate_table)
    return out[None]


def solution(mesh):
    return jax.shard_map(
        body,
        mesh=mesh,
        in_specs=(P("span", "seq", None, None), P("span"), P("span"), P()),
        out_specs=P("span", "seq", None),
        check_vma=False,
    )
```

```python
import math

import jax
import jax.numpy as jnp
from jax import lax
from jax.experimental import pallas as pl
from jax.experimental.pallas import tpu as pltpu
from jax.sharding import PartitionSpec as P

HD = 128
WIN = 2
OWN = 2
SLOTS = OWN + WIN
SOURCES = 16
TOK = 128
ROWS = SOURCES * TOK
CHIPS = 32
PARTS = 4
PART = TOK // PARTS
KEYS = SOURCES * PART
TILE = 256
SHARES = (80, 48)
STARTS = (0, SOURCES * 80)
SCALE = math.log2(math.e) / math.sqrt(HD)
MESH = pl.DeviceIdType.MESH


def device(y, z, x, core):
    return (y * 4 + z % 4, (z // 4) * 8 + x * 2 + core)


def kernel(
    qkv, timestep, offsets, gate_table, out,
    queries, pairs, results, gates, note, notes, row_max, total,
    query_recv, pair_recv, out_recv, note_recv, gate_sem,
    query_send, pair_send, out_send, note_send, chain_send,
    query_near_send, pair_near_send, out_near_send,
):
    span = lax.axis_index("span")
    seq = lax.axis_index("seq")
    y, z_lo = span // 4, span % 4
    z_hi, x, core = seq // 8, seq // 2 % 4, seq % 2
    z = z_hi * 4 + z_lo
    head = x * 8 + z
    home = z_lo // 2
    first_span = y * 4 + core * OWN
    at_home = core == home
    following = device((y + core) % 4, z, x, 1 - core)
    beyond = device((y + 3 + 2 * core) % 4, z, x, 1 - core)

    barrier = pltpu.get_barrier_semaphore()
    greeted = [beyond]
    for turn in range(CHIPS):
        for other in range(2):
            if turn or other:
                greeted.append(device(y, (z + turn) % 8, (x + turn // 8) % 4, (core + other) % 2))
    for other in greeted:
        pl.semaphore_signal(barrier, inc=1, device_id=other, device_id_type=MESH)
    pl.semaphore_wait(barrier, len(greeted))

    def columns(which):
        return pl.ds(pl.multiple_of(which * HD, HD), HD)

    def remote(src, dst, send_sem, recv_sem, target):
        return pltpu.make_async_remote_copy(
            src_ref=src, dst_ref=dst, send_sem=send_sem, recv_sem=recv_sem,
            device_id=target, device_id_type=MESH,
        )

    def here_or_there(stays, src, dst, send_sem, recv_sem, target):
        @pl.when(stays)
        def _():
            pltpu.make_async_copy(src, dst, recv_sem).start()

        @pl.when(jnp.logical_not(stays))
        def _():
            remote(src, dst, send_sem, recv_sem, target).start()

    def wait_bytes(ref, sem):
        pltpu.make_async_copy(ref, ref, sem).wait()

    def scatter(source, dst, send_sem, near_sem, recv_sem):
        here_or_there(at_home, source(head), dst, near_sem, recv_sem, device(y, z, x, home))

        def step(turn, carry):
            to_z, to_x = (z + turn) % 8, (x + turn // 8) % 4
            remote(source(to_x * 8 + to_z), dst, send_sem, recv_sem, device(y, to_z, to_x, home)).start()
            return carry

        lax.fori_loop(1, CHIPS, step, 0)

    mine = z_lo % 2

    def query_rows(share, which):
        size = SHARES[share]
        return pl.ds(pl.multiple_of(STARTS[share] + which * size, 16), size)

    def token_rows(share):
        return pl.ds(share * SHARES[0], SHARES[share])

    def scatter_queries(share):
        scatter(
            lambda which: qkv.at[0, token_rows(share), columns(which)],
            queries.at[mine, query_rows(share, seq), :],
            query_send.at[share], query_near_send.at[share], query_recv.at[share, mine],
        )

    def scatter_pairs(part):
        scatter(
            lambda which: qkv.at[1:3, pl.ds(part * PART, PART), columns(which)],
            pairs.at[part, :, WIN + mine, pl.ds(pl.multiple_of(seq * PART, PART), PART), :],
            pair_send.at[part], pair_near_send.at[part], pair_recv.at[WIN + mine, part],
        )

    def arrived(slot, part):
        wait_bytes(pairs.at[part, :, slot], pair_recv.at[slot, part])

    def pass_on(own, part):
        arrived(WIN + own, part)
        remote(
            pairs.at[part, :, WIN + own], pairs.at[part, :, own],
            chain_send.at[own, part], pair_recv.at[own, part], following,
        ).start()

    def attend(share, own, part):
        three = pl.ds(own, WIN + 1)
        first = first_span + own - WIN
        allowed = [first + step >= notes[own, 1, 0:1, 0:1] for step in range(WIN)]
        keys = pairs[part, 0, three].reshape((WIN + 1) * KEYS, HD)
        values = jnp.concatenate(
            [pairs[part, 1, three].reshape((WIN + 1) * KEYS, HD), jnp.ones(((WIN + 1) * KEYS, HD), jnp.bfloat16)], axis=1
        )
        tiles = SOURCES * SHARES[share] // TILE

        def rows(tile):
            return pl.ds(STARTS[share] + tile * TILE, TILE)

        def scores_of(tile):
            return lax.dot_general(
                queries[own, rows(tile), :], keys, (((1,), (1,)), ((), ())), preferred_element_type=jnp.float32
            )

        def update(tile, scores):
            each = [scores[:, step * KEYS : (step + 1) * KEYS] for step in range(WIN + 1)]
            largest = []
            for block in each:
                most = block[:, :HD]
                for column in range(HD, KEYS, HD):
                    most = jnp.maximum(most, block[:, column : column + HD])
                largest.append(most)
            most = largest[WIN]
            for step in range(WIN):
                most = jnp.maximum(most, jnp.where(allowed[step], largest[step], -1e30))
            old = row_max[own, rows(tile), :]
            new = jnp.maximum(old, jnp.broadcast_to(jnp.max(most, axis=1, keepdims=True), old.shape))
            factor = jnp.exp2((old - new) * SCALE)
            shift = (new * SCALE)[:, :1]
            weights = [
                jnp.exp2(
                    each[step] * jnp.where(allowed[step], jnp.float32(SCALE), 0.0)
                    - jnp.where(allowed[step], shift, 1e30)
                )
                for step in range(WIN)
            ]
            weights.append(jnp.exp2(each[WIN] * SCALE - shift))
            total[own, rows(tile), :] = total[own, rows(tile), :] * jnp.concatenate([factor, factor], axis=1) + jnp.dot(
                jnp.concatenate(weights, axis=1).astype(jnp.bfloat16), values, preferred_element_type=jnp.float32
            )
            row_max[own, rows(tile), :] = new

        scores = scores_of(0)
        for tile in range(tiles):
            later = scores_of(tile + 1) if tile + 1 < tiles else None
            update(tile, scores)
            scores = later

    def finish(share, own):
        size = SHARES[share]
        whole = pl.ds(STARTS[share], SOURCES * size)
        row = lax.broadcasted_iota(jnp.int32, gates.shape, 0) == notes[own, 0, 0:1, 0:1]
        gate = jnp.sum(jnp.where(row, gates[...], 0.0), axis=0, keepdims=True)
        done = total[own, whole, :HD] / total[own, whole, HD:] * gate
        results[pl.ds(pl.multiple_of(own * ROWS + STARTS[share], TILE), SOURCES * size), :] = done.astype(jnp.bfloat16)
        to_z_lo = core * OWN + own

        def block(which):
            return results.at[pl.ds(pl.multiple_of(own * ROWS + STARTS[share] + which * size, 16), size), :]

        dst = out.at[token_rows(share), columns(head)]
        here_or_there(
            z_lo == to_z_lo, block(seq), dst, out_near_send.at[share, own], out_recv,
            device(y, z_hi * 4 + to_z_lo, x, core),
        )

        def step(turn, carry):
            which = (seq + turn) % SOURCES
            target = device(y, which // 8 * 4 + to_z_lo, which // 2 % 4, which % 2)
            remote(block(which), dst, out_send.at[share, own], out_recv, target).start()
            return carry

        lax.fori_loop(1, SOURCES, step, 0)

    note[0] = jnp.full(note.shape[1:], timestep[0], jnp.int32)
    note[1] = jnp.full(note.shape[1:], offsets[0], jnp.int32)
    gate_copy = pltpu.make_async_copy(gate_table.at[:, columns(head)], gates, gate_sem)
    for other in range(2):
        to_z = z_hi * 4 + core * 2 + other
        here_or_there(
            jnp.logical_and(at_home, to_z == z), note, notes.at[mine],
            note_send.at[other], note_recv.at[mine], device(y, to_z, x, home),
        )
    scatter_queries(0)
    for part in range(PARTS):
        scatter_pairs(part)
    scatter_queries(1)
    gate_copy.start()
    row_max[...] = jnp.full_like(row_max, -1e30)
    total[...] = jnp.zeros_like(total)
    gate_copy.wait()

    def queries_here(share):
        for own in range(OWN):
            wait_bytes(
                queries.at[own, pl.ds(STARTS[share], SOURCES * SHARES[share]), :], query_recv.at[share, own]
            )

    for own in range(OWN):
        wait_bytes(notes.at[own], note_recv.at[own])
    queries_here(0)
    pass_on(1, 0)
    pass_on(0, 0)

    def early(index, carry):
        part, own = index // OWN, 1 - index % OWN

        @pl.when(jnp.logical_and(own == 0, part < PARTS - 1))
        def _():
            pass_on(1, part + 1)
            pass_on(0, part + 1)

        arrived(own, part)
        attend(0, own, part)

        @pl.when(part == PARTS - 1)
        def _():
            finish(0, own)

        return carry

    lax.fori_loop(0, PARTS * OWN, early, 0)
    queries_here(1)

    def late(index, carry):
        part, own = index % PARTS, 1 - index // PARTS
        attend(1, own, part)

        @pl.when(part == PARTS - 1)
        def _():
            finish(1, own)

        return carry

    lax.fori_loop(0, PARTS * OWN, late, 0)

    def rows_left(count, sem):
        wait_bytes(results.at[pl.ds(0, count), :], sem)

    for share, size in enumerate(SHARES):
        for own in range(OWN):
            rows_left((SOURCES - 1) * size, out_send.at[share, own])

            @pl.when(z_lo != core * OWN + own)
            def _():
                rows_left(size, out_near_send.at[share, own])

        rows_left((CHIPS - 1) * size, query_send.at[share])
    for part in range(PARTS):
        rows_left((CHIPS - 1) * 2 * PART, pair_send.at[part])
        for own in range(OWN):
            wait_bytes(pairs.at[part, :, own], chain_send.at[own, part])
    for other in range(2):
        @pl.when(jnp.logical_not(jnp.logical_and(at_home, z_hi * 4 + core * 2 + other == z)))
        def _():
            wait_bytes(note, note_send.at[other])

    @pl.when(jnp.logical_not(at_home))
    def _():
        for share, size in enumerate(SHARES):
            rows_left(size, query_near_send.at[share])
        for part in range(PARTS):
            rows_left(2 * PART, pair_near_send.at[part])

    wait_bytes(out, out_recv)


def body(qkv, timestep, offsets, gate_table):
    stacked = jnp.transpose(qkv[0], (1, 0, 2))
    anywhere = pl.BlockSpec(memory_space=pl.ANY)
    scalar = pl.BlockSpec(memory_space=pltpu.SMEM)
    dma = pltpu.SemaphoreType.DMA
    out = pl.pallas_call(
        kernel,
        out_shape=jax.ShapeDtypeStruct((TOK, qkv.shape[3]), jnp.bfloat16),
        in_specs=[anywhere, scalar, scalar, anywhere],
        out_specs=anywhere,
        scratch_shapes=[
            pltpu.VMEM((OWN, ROWS, HD), jnp.bfloat16),
            pltpu.VMEM((PARTS, 2, SLOTS, KEYS, HD), jnp.bfloat16),
            pltpu.VMEM((OWN * ROWS, HD), jnp.bfloat16),
            pltpu.VMEM((gate_table.shape[0], HD), jnp.float32),
            pltpu.VMEM((2, 8, HD), jnp.int32),
            pltpu.VMEM((OWN, 2, 8, HD), jnp.int32),
            pltpu.VMEM((OWN, ROWS, HD), jnp.float32),
            pltpu.VMEM((OWN, ROWS, 2 * HD), jnp.float32),
            dma((2, OWN)),
            dma((SLOTS, PARTS)),
            dma,
            dma((OWN,)),
            dma,
            dma((2,)),
            dma((PARTS,)),
            dma((2, OWN)),
            dma((2,)),
            dma((OWN, PARTS)),
            dma((2,)),
            dma((PARTS,)),
            dma((2, OWN)),
        ],
        compiler_params=pltpu.CompilerParams(
            collective_id=0, has_side_effects=True, vmem_limit_bytes=56 * 1024 * 1024
        ),
        cost_estimate=pl.CostEstimate(
            flops=4 * OWN * ROWS * (WIN + 1) * ROWS * HD,
            bytes_accessed=4 * 1024 * 1024,
            transcendentals=OWN * ROWS * (WIN + 1) * ROWS,
        ),
        name="span_attention",
    )(stacked, timestep, offsets, gate_table)
    return out[None]


def solution(mesh):
    return jax.shard_map(
        body,
        mesh=mesh,
        in_specs=(P("span", "seq", None, None), P("span"), P("span"), P()),
        out_specs=P("span", "seq", None),
        check_vma=False,
    )
```

```python
import math

import jax
import jax.numpy as jnp
from jax import lax
from jax.experimental import pallas as pl
from jax.experimental.pallas import tpu as pltpu
from jax.sharding import PartitionSpec as P

HD = 128
WIN = 2
OWN = 2
SLOTS = OWN + WIN
SOURCES = 16
TOK = 128
ROWS = SOURCES * TOK
CHIPS = 32
PARTS = 4
PART = TOK // PARTS
KEYS = SOURCES * PART
TILE = 256
SHARES = (96, 32)
STARTS = (0, SOURCES * 96)
SCALE = math.log2(math.e) / math.sqrt(HD)
MESH = pl.DeviceIdType.MESH


def device(y, z, x, core):
    return (y * 4 + z % 4, (z // 4) * 8 + x * 2 + core)


def kernel(
    qkv, timestep, offsets, gate_table, out,
    queries, pairs, results, gates, note, notes, row_max, total,
    query_recv, pair_recv, out_recv, note_recv, gate_sem,
    query_send, pair_send, out_send, note_send, chain_send,
    query_near_send, pair_near_send, out_near_send,
):
    span = lax.axis_index("span")
    seq = lax.axis_index("seq")
    y, z_lo = span // 4, span % 4
    z_hi, x, core = seq // 8, seq // 2 % 4, seq % 2
    z = z_hi * 4 + z_lo
    head = x * 8 + z
    home = z_lo // 2
    first_span = y * 4 + core * OWN
    at_home = core == home
    following = device((y + core) % 4, z, x, 1 - core)
    beyond = device((y + 3 + 2 * core) % 4, z, x, 1 - core)

    barrier = pltpu.get_barrier_semaphore()
    greeted = [beyond]
    for turn in range(CHIPS):
        for other in range(2):
            if turn or other:
                greeted.append(device(y, (z + turn) % 8, (x + turn // 8) % 4, (core + other) % 2))
    for other in greeted:
        pl.semaphore_signal(barrier, inc=1, device_id=other, device_id_type=MESH)
    pl.semaphore_wait(barrier, len(greeted))

    def columns(which):
        return pl.ds(pl.multiple_of(which * HD, HD), HD)

    def remote(src, dst, send_sem, recv_sem, target):
        return pltpu.make_async_remote_copy(
            src_ref=src, dst_ref=dst, send_sem=send_sem, recv_sem=recv_sem,
            device_id=target, device_id_type=MESH,
        )

    def here_or_there(stays, src, dst, send_sem, recv_sem, target):
        @pl.when(stays)
        def _():
            pltpu.make_async_copy(src, dst, recv_sem).start()

        @pl.when(jnp.logical_not(stays))
        def _():
            remote(src, dst, send_sem, recv_sem, target).start()

    def wait_bytes(ref, sem):
        pltpu.make_async_copy(ref, ref, sem).wait()

    def scatter(source, dst, send_sem, near_sem, recv_sem):
        here_or_there(at_home, source(head), dst, near_sem, recv_sem, device(y, z, x, home))

        def step(turn, carry):
            to_z, to_x = (z + turn) % 8, (x + turn // 8) % 4
            remote(source(to_x * 8 + to_z), dst, send_sem, recv_sem, device(y, to_z, to_x, home)).start()
            return carry

        lax.fori_loop(1, CHIPS, step, 0)

    mine = z_lo % 2

    def query_rows(share, which):
        size = SHARES[share]
        return pl.ds(pl.multiple_of(STARTS[share] + which * size, 16), size)

    def token_rows(share):
        return pl.ds(share * SHARES[0], SHARES[share])

    def scatter_queries(share):
        scatter(
            lambda which: qkv.at[0, token_rows(share), columns(which)],
            queries.at[mine, query_rows(share, seq), :],
            query_send.at[share], query_near_send.at[share], query_recv.at[share, mine],
        )

    def scatter_pairs(part):
        scatter(
            lambda which: qkv.at[1:3, pl.ds(part * PART, PART), columns(which)],
            pairs.at[part, :, WIN + mine, pl.ds(pl.multiple_of(seq * PART, PART), PART), :],
            pair_send.at[part], pair_near_send.at[part], pair_recv.at[WIN + mine, part],
        )

    def arrived(slot, part):
        wait_bytes(pairs.at[part, :, slot], pair_recv.at[slot, part])

    def pass_on(own, part):
        arrived(WIN + own, part)
        remote(
            pairs.at[part, :, WIN + own], pairs.at[part, :, own],
            chain_send.at[own, part], pair_recv.at[own, part], following,
        ).start()

    def attend(share, own, part):
        three = pl.ds(own, WIN + 1)
        first = first_span + own - WIN
        allowed = [first + step >= notes[own, 1, 0:1, 0:1] for step in range(WIN)]
        keys = pairs[part, 0, three].reshape((WIN + 1) * KEYS, HD)
        values = jnp.concatenate(
            [pairs[part, 1, three].reshape((WIN + 1) * KEYS, HD), jnp.ones(((WIN + 1) * KEYS, HD), jnp.bfloat16)], axis=1
        )
        tiles = SOURCES * SHARES[share] // TILE

        def rows(tile):
            return pl.ds(STARTS[share] + tile * TILE, TILE)

        def scores_of(tile):
            return lax.dot_general(
                queries[own, rows(tile), :], keys, (((1,), (1,)), ((), ())), preferred_element_type=jnp.float32
            )

        def update(tile, scores):
            each = [scores[:, step * KEYS : (step + 1) * KEYS] for step in range(WIN + 1)]
            largest = []
            for block in each:
                most = block[:, :HD]
                for column in range(HD, KEYS, HD):
                    most = jnp.maximum(most, block[:, column : column + HD])
                largest.append(most)
            most = largest[WIN]
            for step in range(WIN):
                most = jnp.maximum(most, jnp.where(allowed[step], largest[step], -1e30))
            old = row_max[own, rows(tile), :]
            new = jnp.maximum(old, jnp.broadcast_to(jnp.max(most, axis=1, keepdims=True), old.shape))
            factor = jnp.exp2((old - new) * SCALE)
            shift = (new * SCALE)[:, :1]
            weights = [
                jnp.exp2(
                    each[step] * jnp.where(allowed[step], jnp.float32(SCALE), 0.0)
                    - jnp.where(allowed[step], shift, 1e30)
                )
                for step in range(WIN)
            ]
            weights.append(jnp.exp2(each[WIN] * SCALE - shift))
            total[own, rows(tile), :] = total[own, rows(tile), :] * jnp.concatenate([factor, factor], axis=1) + jnp.dot(
                jnp.concatenate(weights, axis=1).astype(jnp.bfloat16), values, preferred_element_type=jnp.float32
            )
            row_max[own, rows(tile), :] = new

        scores = scores_of(0)
        for tile in range(tiles):
            later = scores_of(tile + 1) if tile + 1 < tiles else None
            update(tile, scores)
            scores = later

    def finish(share, own):
        size = SHARES[share]
        whole = pl.ds(STARTS[share], SOURCES * size)
        row = lax.broadcasted_iota(jnp.int32, gates.shape, 0) == notes[own, 0, 0:1, 0:1]
        gate = jnp.sum(jnp.where(row, gates[...], 0.0), axis=0, keepdims=True)
        done = total[own, whole, :HD] / total[own, whole, HD:] * gate
        results[pl.ds(pl.multiple_of(own * ROWS + STARTS[share], TILE), SOURCES * size), :] = done.astype(jnp.bfloat16)
        to_z_lo = core * OWN + own

        def block(which):
            return results.at[pl.ds(pl.multiple_of(own * ROWS + STARTS[share] + which * size, 16), size), :]

        dst = out.at[token_rows(share), columns(head)]
        here_or_there(
            z_lo == to_z_lo, block(seq), dst, out_near_send.at[share, own], out_recv,
            device(y, z_hi * 4 + to_z_lo, x, core),
        )

        def step(turn, carry):
            which = (seq + turn) % SOURCES
            target = device(y, which // 8 * 4 + to_z_lo, which // 2 % 4, which % 2)
            remote(block(which), dst, out_send.at[share, own], out_recv, target).start()
            return carry

        lax.fori_loop(1, SOURCES, step, 0)

    note[0] = jnp.full(note.shape[1:], timestep[0], jnp.int32)
    note[1] = jnp.full(note.shape[1:], offsets[0], jnp.int32)
    gate_copy = pltpu.make_async_copy(gate_table.at[:, columns(head)], gates, gate_sem)
    for other in range(2):
        to_z = z_hi * 4 + core * 2 + other
        here_or_there(
            jnp.logical_and(at_home, to_z == z), note, notes.at[mine],
            note_send.at[other], note_recv.at[mine], device(y, to_z, x, home),
        )
    scatter_queries(0)
    for part in range(PARTS):
        scatter_pairs(part)
    scatter_queries(1)
    gate_copy.start()
    row_max[...] = jnp.full_like(row_max, -1e30)
    total[...] = jnp.zeros_like(total)
    gate_copy.wait()

    def queries_here(share):
        for own in range(OWN):
            wait_bytes(
                queries.at[own, pl.ds(STARTS[share], SOURCES * SHARES[share]), :], query_recv.at[share, own]
            )

    for own in range(OWN):
        wait_bytes(notes.at[own], note_recv.at[own])
    queries_here(0)
    pass_on(1, 0)
    pass_on(0, 0)

    def early(index, carry):
        part, own = index // OWN, 1 - index % OWN

        @pl.when(jnp.logical_and(own == 0, part < PARTS - 1))
        def _():
            pass_on(1, part + 1)
            pass_on(0, part + 1)

        arrived(own, part)
        attend(0, own, part)

        @pl.when(part == PARTS - 1)
        def _():
            finish(0, own)

        return carry

    lax.fori_loop(0, PARTS * OWN, early, 0)
    queries_here(1)

    def late(index, carry):
        part, own = index % PARTS, 1 - index // PARTS
        attend(1, own, part)

        @pl.when(part == PARTS - 1)
        def _():
            finish(1, own)

        return carry

    lax.fori_loop(0, PARTS * OWN, late, 0)

    def rows_left(count, sem):
        wait_bytes(results.at[pl.ds(0, count), :], sem)

    for share, size in enumerate(SHARES):
        for own in range(OWN):
            rows_left((SOURCES - 1) * size, out_send.at[share, own])

            @pl.when(z_lo != core * OWN + own)
            def _():
                rows_left(size, out_near_send.at[share, own])

        rows_left((CHIPS - 1) * size, query_send.at[share])
    for part in range(PARTS):
        rows_left((CHIPS - 1) * 2 * PART, pair_send.at[part])
        for own in range(OWN):
            wait_bytes(pairs.at[part, :, own], chain_send.at[own, part])
    for other in range(2):
        @pl.when(jnp.logical_not(jnp.logical_and(at_home, z_hi * 4 + core * 2 + other == z)))
        def _():
            wait_bytes(note, note_send.at[other])

    @pl.when(jnp.logical_not(at_home))
    def _():
        for share, size in enumerate(SHARES):
            rows_left(size, query_near_send.at[share])
        for part in range(PARTS):
            rows_left(2 * PART, pair_near_send.at[part])

    wait_bytes(out, out_recv)


def body(qkv, timestep, offsets, gate_table):
    stacked = jnp.transpose(qkv[0], (1, 0, 2))
    anywhere = pl.BlockSpec(memory_space=pl.ANY)
    scalar = pl.BlockSpec(memory_space=pltpu.SMEM)
    dma = pltpu.SemaphoreType.DMA
    out = pl.pallas_call(
        kernel,
        out_shape=jax.ShapeDtypeStruct((TOK, qkv.shape[3]), jnp.bfloat16),
        in_specs=[anywhere, scalar, scalar, anywhere],
        out_specs=anywhere,
        scratch_shapes=[
            pltpu.VMEM((OWN, ROWS, HD), jnp.bfloat16),
            pltpu.VMEM((PARTS, 2, SLOTS, KEYS, HD), jnp.bfloat16),
            pltpu.VMEM((OWN * ROWS, HD), jnp.bfloat16),
            pltpu.VMEM((gate_table.shape[0], HD), jnp.float32),
            pltpu.VMEM((2, 8, HD), jnp.int32),
            pltpu.VMEM((OWN, 2, 8, HD), jnp.int32),
            pltpu.VMEM((OWN, ROWS, HD), jnp.float32),
            pltpu.VMEM((OWN, ROWS, 2 * HD), jnp.float32),
            dma((2, OWN)),
            dma((SLOTS, PARTS)),
            dma,
            dma((OWN,)),
            dma,
            dma((2,)),
            dma((PARTS,)),
            dma((2, OWN)),
            dma((2,)),
            dma((OWN, PARTS)),
            dma((2,)),
            dma((PARTS,)),
            dma((2, OWN)),
        ],
        compiler_params=pltpu.CompilerParams(
            collective_id=0, has_side_effects=True, vmem_limit_bytes=56 * 1024 * 1024
        ),
        cost_estimate=pl.CostEstimate(
            flops=4 * OWN * ROWS * (WIN + 1) * ROWS * HD,
            bytes_accessed=4 * 1024 * 1024,
            transcendentals=OWN * ROWS * (WIN + 1) * ROWS,
        ),
        name="span_attention",
    )(stacked, timestep, offsets, gate_table)
    return out[None]


def solution(mesh):
    return jax.shard_map(
        body,
        mesh=mesh,
        in_specs=(P("span", "seq", None, None), P("span"), P("span"), P()),
        out_specs=P("span", "seq", None),
        check_vma=False,
    )
```
